128 devices in a mesh: dp: 8 (over y, core), mp: 16 (over z, x).
Axes of the slice: x: 4, y: 4, z: 4, core: 2. Of those that a mesh axis runs over, the one named last changes fastest.
Arguments:
- momentum: bfloat16 [8, 5120, 12800], P('dp', None, 'mp'), may hold values from -80 to 80
- gradient: bfloat16 [8, 5120, 12800], P('dp', None, 'mp'), may hold values from -80 to 80
- right_factor: bfloat16 [12800, 128], P('mp'), may hold values from -6 to 6
Outputs:
- momentum_next: bfloat16 [8, 5120, 12800], P('dp', None, 'mp')
- left_factor: bfloat16 [5120, 128], replicated
- right_next: bfloat16 [12800, 128], P('mp')
The draws below stay inside these ranges and needn't reach their ends.
All inputs are finite; a program needn't handle non-finite values.
Results may differ from the reference program's by a relative error of at most 0.017.
Values may be sent and summed in bfloat16 or wider, within the bound.
A program may use at most 128 MiB of HBM per device.

```python
import math
import jax
import jax.numpy as jnp
from jax import lax

D = 5120
RANK = 128
HID = 12800
N_DP = 8


def shared_parts(key):
    keys = jax.random.split(jax.random.fold_in(key, 11), 5)
    rows = jnp.exp(jax.random.uniform(keys[0], (D, 1), jnp.float32, math.log(0.3), math.log(3.0)))
    ramp = jnp.arange(HID, dtype=jnp.float32) / HID - 0.5
    cols = jnp.exp(jax.random.uniform(keys[1], (1, HID), jnp.float32, math.log(0.3), math.log(3.3)))
    cols = cols * jnp.exp(math.log(3.0) * ramp)[None, :]
    inner = max(RANK // 2, 1)
    left_part = jax.random.normal(keys[2], (D, inner), jnp.float32)
    right_part = jax.random.normal(keys[3], (inner, HID), jnp.float32)
    weights = jnp.exp(jax.random.uniform(keys[4], (1, inner), jnp.float32, 0.0, math.log(2.0)))
    shared = jnp.dot(left_part * weights, right_part, precision=lax.Precision.HIGHEST)
    shared = shared / (1.47 * math.sqrt(inner))
    return (rows, cols, shared)


def base_values(key, shape, spread):
    return jax.random.truncated_normal(key, -4.0, 4.0, shape, jnp.float32) * spread


def combine(shared, noise, weight, rows, cols):
    values = jnp.clip(weight * shared[None] + noise, -4.5, 4.5)
    return (values * rows[None] * cols[None]).astype(jnp.bfloat16)


def draw_momentum(key, part):
    rows, cols, shared = shared_parts(key)
    key = jax.random.fold_in(key, 1)
    noise = base_values(key, (N_DP, D, HID), 0.35)
    return combine(shared, noise, 0.9, rows, cols)


def draw_gradient(key, part):
    rows, cols, shared = shared_parts(key)
    key = jax.random.fold_in(key, 2)
    noise = base_values(key, (N_DP, D, HID), 0.25)
    return combine(shared, noise, 0.6, rows, cols)


def block_levels(stream_key, extent, cuts, smallest, largest):
    factor_of = 1.0
    for axis_at, blocks in cuts:
        heights = jax.random.uniform(jax.random.fold_in(jax.random.fold_in(stream_key, 6), axis_at), (blocks,), jnp.float32, smallest / len(cuts), largest / len(cuts))
        factor_of = factor_of * jnp.repeat(jnp.exp(heights), extent[axis_at] // blocks).reshape((-1,) + (1,) * (len(extent) - 1 - axis_at))
    return factor_of


def centred(key, extent, scale, reach, cuts=(), kind=jnp.bfloat16):
    gain = block_levels(key, extent, cuts, -0.22, 0.18) if cuts else 1.0
    drawn = jax.random.normal(key, extent, jnp.float32) * scale * gain
    return jnp.minimum(jnp.maximum(drawn, -reach), reach).astype(kind)


def setup_inputs(seed: int = 0) -> dict:
    splits = jax.random.split(jax.random.key(seed), 4)
    momentum = draw_momentum(jax.random.fold_in(splits[3], 71), 0)
    gradient = draw_gradient(jax.random.fold_in(splits[3], 71), 0)
    right_factor = centred(splits[2], (HID, RANK), 1.0, 6.0, ((0, 16),))
    return {"momentum": momentum, "gradient": gradient, "right_factor": right_factor}


DECAY = 0.9

def blended(pair):
    return (pair[0].astype(jnp.float32) + pair[1].astype(jnp.float32)).astype(jnp.bfloat16)

def reference(momentum, gradient, right_factor):

    def left_term(carry, pair):
        blend = blended(pair)
        return (carry + jnp.dot(blend.astype(jnp.float32), right_factor.astype(jnp.float32), preferred_element_type=jnp.float32), None)
    left_total, _ = lax.scan(left_term, jnp.zeros((D, RANK), jnp.float32), (momentum, gradient))
    mean_left = left_total / N_DP
    gram = jnp.dot(mean_left.T, mean_left, precision=lax.Precision.HIGHEST) / D
    lower = jnp.linalg.cholesky(gram)
    orthed = lax.linalg.triangular_solve(lower, mean_left, left_side=False, lower=True, transpose_a=True)
    left_factor = orthed.astype(jnp.bfloat16)

    def right_term(carry, pair):
        blend = blended(pair)
        term = lax.dot_general(blend.astype(jnp.float32), left_factor.astype(jnp.float32), (((0,), (0,)), ((), ())), preferred_element_type=jnp.float32)
        return (carry + term, None)
    right_total, _ = lax.scan(right_term, jnp.zeros((HID, RANK), jnp.float32), (momentum, gradient))
    mean_right = right_total / (N_DP * jnp.sqrt(jnp.float32(D)))
    scale = jnp.sqrt(lax.optimization_barrier(jnp.sum(mean_right * mean_right, axis=0)) / HID + 1e-06)
    right_next = (mean_right / scale).astype(jnp.bfloat16)
    right_round = mean_right.astype(jnp.bfloat16)
    coef = (1.0 - DECAY) / jnp.sqrt(jnp.float32(D))

    def feedback(pair):
        blend = blended(pair)
        low = jnp.dot(left_factor.astype(jnp.float32), right_round.T.astype(jnp.float32), preferred_element_type=jnp.float32)
        return (blend.astype(jnp.float32) - coef * low).astype(jnp.bfloat16)
    momentum_next = lax.map(feedback, (momentum, gradient))
    return (momentum_next, left_factor, right_next)
```

```python
import functools
import math

import jax
import jax.numpy as jnp
from jax import lax
from jax.experimental import pallas as pl
from jax.experimental.pallas import tpu as pltpu
from jax.sharding import PartitionSpec as P

D = 5120
RANK = 128
DECAY = 0.9
EPS = 1e-06
MESH = pl.DeviceIdType.MESH
F32 = jnp.float32
BF16 = jnp.bfloat16

CHUNK = 256
N_CHUNKS = D // CHUNK
PARTS = ((0, 8, (0, 1, 2)), (8, 7, (1, 2, 0)), (15, 5, (2, 0, 1)))
STAGES = 7


def device(pos, core):
    return (pos[1] * 2 + core, pos[2] * 4 + pos[0])


def moved(pos, axis, steps):
    at = list(pos)
    at[axis] = lax.rem(pos[axis] + steps, 4)
    return at


def rows_at(start, size):
    return pl.ds(pl.multiple_of(start, 8), size)


def lanes_at(start, size):
    return pl.ds(pl.multiple_of(start, 128), size)


def split(value):
    high = value.astype(BF16)
    return high, (value - high.astype(F32)).astype(BF16)


BLOCK = 4


def eliminate(tiles, k, lane, sub):
    first, shift = k // 8, k % 8
    groups = range(first, RANK // 8)

    def lanes(tile, j):
        return jnp.broadcast_to(tile[:, j : j + 1], (8, RANK))

    def row(tile, i):
        return jnp.broadcast_to(tile[i : i + 1, :], (8, RANK))

    col = [{g: lanes(tiles[g], k + j) for g in groups} for j in range(BLOCK)]
    rows = [row(tiles[first], shift + i) for i in range(BLOCK)]
    piv = [[row(col[j][first], shift + i) for j in range(BLOCK)] for i in range(BLOCK)]
    mult = []
    done = []
    pivots = []
    for j in range(BLOCK):
        inverse = 1.0 / piv[j][j]
        pivots.append(piv[j][j])
        done.append(jnp.where(lane == k + j, 1.0, rows[j]))
        for i in range(j + 1, BLOCK):
            factor = piv[i][j] * inverse
            rows[i] = jnp.where(lane == k + j, 0.0, rows[i]) - factor * done[j]
            for m in range(j + 1, BLOCK):
                piv[i][m] = piv[i][m] - factor * piv[j][m]
        mult.append({g: col[j][g] * inverse for g in groups})
        for m in range(j + 1, BLOCK):
            for g in groups:
                col[m][g] = col[m][g] - mult[j][g] * piv[j][m]
    inside = (lane >= k) & (lane < k + BLOCK)
    last = [
        jnp.where((lane > k + j) & (lane < k + BLOCK), 0.0, done[j]) for j in range(BLOCK)
    ]
    for g in groups:
        new = jnp.where(inside, 0.0, tiles[g])
        for j in range(BLOCK):
            new = new - mult[j][g] * last[j]
        if g == first:
            new = jnp.where(sub < shift + BLOCK, tiles[g], new)
            for j in range(BLOCK):
                new = jnp.where(sub == shift + j, done[j], new)
        tiles[g] = new
    return pivots


def factor_steps(t_ref, root_ref, begin, end):
    lane = lax.broadcasted_iota(jnp.int32, (8, RANK), 1)
    sub = lax.broadcasted_iota(jnp.int32, (8, RANK), 0)
    tiles = [t_ref[8 * g : 8 * g + 8, :] for g in range(RANK // 8)]
    for k in range(begin, end, BLOCK):
        pivots = eliminate(tiles, k, lane, sub)
        for j in range(BLOCK):
            root_ref[k + j : k + j + 1, :] = lax.rsqrt(pivots[j])[0:1, :]
    for g in range(RANK // 8):
        t_ref[8 * g : 8 * g + 8, :] = tiles[g]


def make_kernel(hid, r_rows):
    def kernel(
        mom_hbm, grad_hbm, right_ref,
        blend_hbm, left_hbm, next_ref, round_ref,
        blend, grad, right_t, part_sum, total, pairs, pairs_t, acc_r, acc_g, left_buf,
        from_core, got1, got2, own2, got3,
        r_part, r_core, r_sum, r_y, r_all, t_ref, root_ref, sq_buf,
        load_sem, send_sem, recv_sem, out_sem, r_send, r_recv, sq_send, sq_recv,
    ):
        dp = lax.axis_index("dp")
        mp = lax.axis_index("mp")
        core = lax.rem(dp, 2)
        pos = (lax.rem(mp, 4), dp // 2, mp // 4)
        sibling = device(pos, 1 - core)

        def load(i, what):
            src, dst = ((mom_hbm, blend), (grad_hbm, grad))[what]
            return pltpu.make_async_copy(
                src.at[0, :, lanes_at(i * CHUNK, CHUNK)],
                dst.at[:, lanes_at(i * CHUNK, CHUNK)],
                load_sem.at[what, i],
            )

        def start_load(i, _):
            load(i, 0).start()
            load(i, 1).start()
            return 0

        lax.fori_loop(0, N_CHUNKS, start_load, 0)

        right_t[...] = right_ref[...].astype(F32).T.astype(BF16)
        barrier = pltpu.get_barrier_semaphore()
        greet = [sibling]
        greet += [device(moved(pos, a, r), core) for a in range(3) for r in range(1, 4)]
        greet += [
            device(moved(moved(pos, 0, r), 2, s), core) for r in range(1, 4) for s in range(1, 4)
        ]
        for peer in greet:
            pl.semaphore_signal(barrier, inc=1, device_id=peer, device_id_type=MESH)

        def remote(src, dst, send, recv, peer):
            return pltpu.make_async_remote_copy(
                src_ref=src, dst_ref=dst, send_sem=send, recv_sem=recv,
                device_id=peer, device_id_type=MESH,
            )

        def took(ref, sem):
            pltpu.make_async_copy(ref, ref, sem).wait()

        def left_chunks(begin, end):
            def one(i, _):
                load(i, 0).wait()
                load(i, 1).wait()
                at = lanes_at(i * CHUNK, CHUNK)
                value = (blend[:, at].astype(F32) + grad[:, at].astype(F32)).astype(BF16)
                blend[:, at] = value
                terms = jnp.dot(right_t[...], value, preferred_element_type=F32)
                for t in range(CHUNK // 128):
                    rows = rows_at(i * CHUNK + t * 128, 128)
                    part_sum[rows, :] = terms[:, t * 128 : (t + 1) * 128]
                return 0

            lax.fori_loop(begin, end, one, 0)

        def geometry(p):
            begin, chunks, axes = PARTS[p]
            half = chunks * CHUNK // 2
            base = begin * CHUNK
            own = base + core * half
            quarter = half // 4
            small = quarter // 4
            return base, half, own, quarter, small, axes

        def core_send(p):
            base, half, own, quarter, small, axes = geometry(p)
            other = base + (1 - core) * half
            remote(
                part_sum.at[rows_at(other, half)], from_core.at[pl.ds(base // 2, half)],
                send_sem.at[p, 0], recv_sem.at[p, 0], sibling,
            ).start()

        def axis_send(p):
            base, half, own, quarter, small, axes = geometry(p)
            took(from_core.at[pl.ds(base // 2, half)], recv_sem.at[p, 0])
            step = 128
            for r in range(0, half, step):
                size = min(step, half - r)
                part_sum[rows_at(own + r, size), :] += from_core[pl.ds(base // 2 + r, size), :]
            for r in range(1, 4):
                to = lax.rem(pos[axes[0]] + r, 4)
                remote(
                    part_sum.at[rows_at(own + to * quarter, quarter)],
                    got1.at[r - 1, pl.ds(base // 8, quarter)],
                    send_sem.at[p, 1], recv_sem.at[p, 1], device(moved(pos, axes[0], r), core),
                ).start()

        def second_send(p):
            base, half, own, quarter, small, axes = geometry(p)
            here = pl.ds(base // 8, quarter)
            took(got1.at[:, here], recv_sem.at[p, 1])
            mine = rows_at(own + pos[axes[0]] * quarter, quarter)
            got1[0, here, :] = (part_sum[mine, :] + got1[0, here, :]) + (
                got1[1, here, :] + got1[2, here, :]
            )
            for r in range(1, 4):
                to = lax.rem(pos[axes[1]] + r, 4)
                remote(
                    got1.at[0, rows_at(base // 8 + to * small, small)],
                    got2.at[r - 1, pl.ds(base // 32, small)],
                    send_sem.at[p, 2], recv_sem.at[p, 2], device(moved(pos, axes[1], r), core),
                ).start()

        def third_send(p):
            base, half, own, quarter, small, axes = geometry(p)
            here = pl.ds(base // 32, small)
            took(got2.at[:, here], recv_sem.at[p, 2])
            mine = rows_at(base // 8 + pos[axes[1]] * small, small)
            own2[here, :] = (got1[0, mine, :] + got2[0, here, :]) + (
                got2[1, here, :] + got2[2, here, :]
            )
            me = pos[axes[2]]
            for r in range(1, 4):
                remote(
                    own2.at[here],
                    got3.at[r - 1, here],
                    send_sem.at[p, 3], recv_sem.at[p, 3], device(moved(pos, axes[2], r), core),
                ).start()

        def gather_send(p):
            base, half, own, quarter, small, axes = geometry(p)
            here = pl.ds(base // 32, small)
            took(got3.at[:, here], recv_sem.at[p, 3])
            me = pos[axes[2]]
            terms = [own2[here, :]] + [got3[r, here, :] for r in range(3)]

            def at_place(j):
                value = terms[0]
                for r in range(1, 4):
                    value = jnp.where(lax.rem(me + 4 - r, 4) == j, terms[r], value)
                return value

            mine = rows_at(own + pos[axes[0]] * quarter + pos[axes[1]] * small, small)
            total[mine, :] = (at_place(0) + at_place(1)) + (at_place(2) + at_place(3))
            for r in range(1, 4):
                remote(
                    total.at[mine], total.at[mine],
                    send_sem.at[p, 4], recv_sem.at[p, 4], device(moved(pos, axes[1], r), core),
                ).start()

        def gather_axis(p):
            base, half, own, quarter, small, axes = geometry(p)
            took(total.at[pl.ds(0, 3 * small)], recv_sem.at[p, 4])
            mine = rows_at(own + pos[axes[0]] * quarter, quarter)
            for r in range(1, 4):
                remote(
                    total.at[mine], total.at[mine],
                    send_sem.at[p, 5], recv_sem.at[p, 5], device(moved(pos, axes[0], r), core),
                ).start()

        def gather_core(p):
            base, half, own, quarter, small, axes = geometry(p)
            took(total.at[pl.ds(0, 3 * quarter)], recv_sem.at[p, 5])
            mine = rows_at(own, half)
            remote(
                total.at[mine], total.at[mine], send_sem.at[p, 6], recv_sem.at[p, 6], sibling
            ).start()

        def use_part(p):
            base, half, own, quarter, small, axes = geometry(p)
            took(total.at[pl.ds(0, half)], recv_sem.at[p, 6])
            size = 2 * half

            def one(i, _):
                at = rows_at(base + i * 128, 128)
                value = total[at, :]
                high, low = split(value)
                cols = lanes_at(i * 128, 128)
                pairs_t[0:RANK, cols] = high
                pairs_t[RANK : 2 * RANK, cols] = low
                high, low = split(value.T)
                pairs[at, 0:RANK] = high
                pairs[at, RANK : 2 * RANK] = low
                return 0

            lax.fori_loop(0, size // 128, one, 0)
            rows = pl.ds(base, size)
            terms = pairs[rows, :]
            gram = jnp.dot(pairs_t[:, 0:size], terms, preferred_element_type=F32)
            acc_g[...] = gram if p == 0 else acc_g[...] + gram
            value = jnp.dot(blend[:, rows], terms, preferred_element_type=F32)
            acc_r[...] = value if p == 0 else acc_r[...] + value

        def sent(p):
            base, half, own, quarter, small, axes = geometry(p)
            took(total.at[pl.ds(0, half)], send_sem.at[p, 0])
            took(total.at[pl.ds(0, 3 * quarter)], send_sem.at[p, 1])
            took(total.at[pl.ds(0, 3 * small)], send_sem.at[p, 2])
            took(total.at[pl.ds(0, 3 * small)], send_sem.at[p, 3])
            took(total.at[pl.ds(0, 3 * small)], send_sem.at[p, 4])
            took(total.at[pl.ds(0, 3 * quarter)], send_sem.at[p, 5])
            took(total.at[pl.ds(0, half)], send_sem.at[p, 6])

        with jax.named_scope("left_product"):
            left_chunks(0, 8)
        with jax.named_scope("barrier"):
            pl.semaphore_wait(barrier, len(greet))
        core_send(0)
        with jax.named_scope("left_product"):
            left_chunks(8, 12)
        axis_send(0)
        with jax.named_scope("left_product"):
            left_chunks(12, 15)
        core_send(1)
        with jax.named_scope("left_product"):
            left_chunks(15, 18)
        axis_send(1)
        with jax.named_scope("left_product"):
            left_chunks(18, 20)
        core_send(2)
        keep = pltpu.make_async_copy(blend, blend_hbm, out_sem.at[0])
        keep.start()
        with jax.named_scope("axis_send"):
            axis_send(2)
        for name, stage in (
            ("second_send", second_send), ("third_send", third_send),
            ("gather_send", gather_send), ("gather_axis", gather_axis),
        ):
            for p in range(3):
                with jax.named_scope(name + str(p)):
                    stage(p)
        with jax.named_scope("gather_core"):
            gather_core(0)
            gather_core(1)
        with jax.named_scope("use_part0"):
            use_part(0)
        with jax.named_scope("gather_core2"):
            gather_core(2)
        with jax.named_scope("use_part1"):
            use_part(1)
        with jax.named_scope("use_part2"):
            use_part(2)

        r_part[0:hid, :] = acc_r[:, 0:RANK] + acc_r[:, RANK : 2 * RANK]
        r_part[hid:, :] = jnp.zeros((r_rows - hid, RANK), F32)
        half_rows = r_rows // 2
        remote(
            r_part.at[rows_at((1 - core) * half_rows, half_rows)], r_core,
            r_send.at[0], r_recv.at[0], sibling,
        ).start()
        t_ref[...] = (acc_g[0:RANK, 0:RANK] + acc_g[RANK:, 0:RANK]) + (
            acc_g[0:RANK, RANK:] + acc_g[RANK:, RANK:]
        )
        with jax.named_scope("factor_steps0"):
            factor_steps(t_ref, root_ref, 0, 16)
        with jax.named_scope("r_core_wait"):
            took(r_core, r_recv.at[0])
        own_half = rows_at(core * half_rows, half_rows)
        r_sum[...] = r_part[own_half, :] + r_core[...]
        piece = half_rows // 4
        for r in range(1, 4):
            to = lax.rem(pos[1] + r, 4)
            remote(
                r_sum.at[rows_at(to * piece, piece)], r_y.at[r - 1],
                r_send.at[1], r_recv.at[1], device(moved(pos, 1, r), core),
            ).start()
        with jax.named_scope("factor_steps16"):
            factor_steps(t_ref, root_ref, 16, 56)
        with jax.named_scope("r_y_wait"):
            took(r_y, r_recv.at[1])
        took(r_core, r_send.at[0])
        mine = rows_at(core * half_rows + pos[1] * piece, piece)
        r_all[mine, :] = (r_sum[rows_at(pos[1] * piece, piece), :] + r_y[0]) + (r_y[1] + r_y[2])
        for r in range(1, 4):
            remote(
                r_all.at[mine], r_all.at[mine],
                r_send.at[2], r_recv.at[2], device(moved(pos, 1, r), core),
            ).start()
        with jax.named_scope("factor_steps56"):
            factor_steps(t_ref, root_ref, 56, 96)
        with jax.named_scope("r_y_gather_wait"):
            took(r_y, r_recv.at[2])
        remote(
            r_all.at[own_half], r_all.at[own_half], r_send.at[3], r_recv.at[3], sibling
        ).start()
        with jax.named_scope("factor_steps96"):
            factor_steps(t_ref, root_ref, 96, RANK)
        lane = lax.broadcasted_iota(jnp.int32, (RANK, RANK), 1)
        sub = lax.broadcasted_iota(jnp.int32, (RANK, RANK), 0)
        lower = jnp.where(lane < sub, t_ref[...], jnp.where(lane == sub, 1.0, 0.0)) * root_ref[...]
        with jax.named_scope("r_core_gather_wait"):
            took(r_core, r_recv.at[3])
        lower_t = lower.T
        mean = jnp.dot(
            r_all[0:hid, :], lower_t, precision=lax.Precision.HIGHEST, preferred_element_type=F32
        ) * F32(0.125)
        round_ref[...] = mean.astype(BF16)
        squares = jnp.broadcast_to(jnp.sum(mean * mean, axis=0, keepdims=True), (8, RANK))
        sq_buf[mp] = squares
        for s in range(4):
            for r in range(4):
                if r or s:
                    remote(
                        sq_buf.at[mp], sq_buf.at[mp], sq_send.at[0], sq_recv.at[0],
                        device(moved(moved(pos, 0, r), 2, s), core),
                    ).start()

        high, low = split(lower_t)
        both = jnp.concatenate([high, low], axis=1)
        weights = jnp.concatenate([both, both], axis=0)
        root = F32(math.sqrt(D))

        def left_rows(i, _):
            at = rows_at(i * CHUNK, CHUNK)
            value = jnp.dot(pairs[at, :], weights, preferred_element_type=F32)
            left_buf[at, :] = ((value[:, :RANK] + value[:, RANK:]) * root).astype(BF16)
            return 0

        with jax.named_scope("left_rows"):
            lax.fori_loop(0, N_CHUNKS, left_rows, 0)
        left_out = pltpu.make_async_copy(left_buf, left_hbm, out_sem.at[1])
        left_out.start()
        with jax.named_scope("squares_wait"):
            took(sq_buf.at[pl.ds(0, 15)], sq_recv.at[0])
        all_squares = sq_buf[0]
        for i in range(1, 16):
            all_squares = all_squares + sq_buf[i]
        scale = jnp.sqrt(all_squares[0:1, :] / (hid * 16) + EPS)
        next_ref[...] = (mean / scale).astype(BF16)

        took(sq_buf.at[pl.ds(0, 15)], sq_send.at[0])
        took(r_y, r_send.at[1])
        took(r_y, r_send.at[2])
        took(r_core, r_send.at[3])
        for p in range(3):
            sent(p)
        left_out.wait()
        keep.wait()

    return kernel


def factors(momentum, gradient, right_factor):
    hid = momentum.shape[1]
    r_rows = -(-hid // 64) * 64
    vmem = pl.BlockSpec(memory_space=pltpu.VMEM)
    hbm = pl.BlockSpec(memory_space=pl.ANY)
    return pl.pallas_call(
        make_kernel(hid, r_rows),
        out_shape=(
            jax.ShapeDtypeStruct((hid, D), BF16),
            jax.ShapeDtypeStruct((D, RANK), BF16),
            jax.ShapeDtypeStruct((hid, RANK), BF16),
            jax.ShapeDtypeStruct((hid, RANK), BF16),
        ),
        in_specs=[hbm, hbm, vmem],
        out_specs=(hbm, hbm, vmem, vmem),
        scratch_shapes=[
            pltpu.VMEM((hid, D), BF16),
            pltpu.VMEM((hid, D), BF16),
            pltpu.VMEM((RANK, hid), BF16),
            pltpu.VMEM((D, RANK), F32),
            pltpu.VMEM((D, RANK), F32),
            pltpu.VMEM((D, 2 * RANK), BF16),
            pltpu.VMEM((2 * RANK, 8 * CHUNK), BF16),
            pltpu.VMEM((hid, 2 * RANK), F32),
            pltpu.VMEM((2 * RANK, 2 * RANK), F32),
            pltpu.VMEM((D, RANK), BF16),
            pltpu.VMEM((D // 2, RANK), F32),
            pltpu.VMEM((3, D // 8, RANK), F32),
            pltpu.VMEM((3, D // 32, RANK), F32),
            pltpu.VMEM((D // 32, RANK), F32),
            pltpu.VMEM((3, D // 32, RANK), F32),
            pltpu.VMEM((r_rows, RANK), F32),
            pltpu.VMEM((r_rows // 2, RANK), F32),
            pltpu.VMEM((r_rows // 2, RANK), F32),
            pltpu.VMEM((3, r_rows // 8, RANK), F32),
            pltpu.VMEM((r_rows, RANK), F32),
            pltpu.VMEM((RANK, RANK), F32),
            pltpu.VMEM((RANK, RANK), F32),
            pltpu.VMEM((16, 8, RANK), F32),
            pltpu.SemaphoreType.DMA((2, N_CHUNKS)),
            pltpu.SemaphoreType.DMA((3, STAGES)),
            pltpu.SemaphoreType.DMA((3, STAGES)),
            pltpu.SemaphoreType.DMA((2,)),
            pltpu.SemaphoreType.DMA((4,)),
            pltpu.SemaphoreType.DMA((4,)),
            pltpu.SemaphoreType.DMA((1,)),
            pltpu.SemaphoreType.DMA((1,)),
        ],
        compiler_params=pltpu.CompilerParams(
            collective_id=0, has_side_effects=True, vmem_limit_bytes=60 << 20
        ),
        name="factors",
    )(momentum, gradient, right_factor)


def feedback_kernel(blend_ref, left_ref, round_ref, out_ref):
    low = lax.dot_general(
        round_ref[...], left_ref[...], (((1,), (1,)), ((), ())), preferred_element_type=F32
    )
    coef = F32((1.0 - DECAY) / math.sqrt(D))
    out_ref[0] = (blend_ref[...].astype(F32) - coef * low).astype(BF16)


def feedback(blend, left_factor, right_round):
    hid = blend.shape[0]
    cols = 512
    return pl.pallas_call(
        feedback_kernel,
        grid=(D // cols,),
        out_shape=jax.ShapeDtypeStruct((1, hid, D), BF16),
        in_specs=[
            pl.BlockSpec((hid, cols), lambda i: (0, i)),
            pl.BlockSpec((cols, RANK), lambda i: (i, 0)),
            pl.BlockSpec((hid, RANK), lambda i: (0, 0)),
        ],
        out_specs=pl.BlockSpec((1, hid, cols), lambda i: (0, 0, i)),
        compiler_params=pltpu.CompilerParams(vmem_limit_bytes=60 << 20),
        name="feedback",
    )(blend, left_factor, right_round)


def shards(momentum, gradient, right_factor):
    blend, left_factor, right_next, right_round = factors(
        momentum.swapaxes(1, 2), gradient.swapaxes(1, 2), right_factor
    )
    momentum_next = feedback(blend, left_factor, right_round).swapaxes(1, 2)
    return momentum_next, left_factor, right_next


def solution(mesh):
    placed = (P("dp", None, "mp"), P("dp", None, "mp"), P("mp", None))
    return jax.shard_map(
        shards,
        mesh=mesh,
        in_specs=placed,
        out_specs=(P("dp", None, "mp"), P(), P("mp", None)),
        check_vma=False,
    )
```

```python
import functools
import math

import jax
import jax.numpy as jnp
from jax import lax
from jax.experimental import pallas as pl
from jax.experimental.pallas import tpu as pltpu
from jax.sharding import PartitionSpec as P

D = 5120
RANK = 128
DECAY = 0.9
EPS = 1e-06
MESH = pl.DeviceIdType.MESH
F32 = jnp.float32
BF16 = jnp.bfloat16
NT = (((1,), (1,)), ((), ()))

CHUNK = 512
N_CHUNKS = D // CHUNK
PARTS = ((0, 4, (0, 1, 2)), (4, 3, (1, 2, 0)), (7, 3, (2, 0, 1)))
STAGES = 7


def device(pos, core):
    return (pos[1] * 2 + core, pos[2] * 4 + pos[0])


def moved(pos, axis, steps):
    at = list(pos)
    at[axis] = lax.rem(pos[axis] + steps, 4)
    return at


def rows_at(start, size):
    return pl.ds(pl.multiple_of(start, 8), size)


def lanes_at(start, size):
    return pl.ds(pl.multiple_of(start, 128), size)


def rows_at16(start, size):
    return pl.ds(pl.multiple_of(start, 16), size)


def split(value):
    high = value.astype(BF16)
    return high, (value - high.astype(F32)).astype(BF16)


BLOCK = 8


def eliminate(tiles, k, lane, sub):
    first, shift = k // 8, k % 8
    groups = range(first, RANK // 8)

    def lanes(tile, j):
        return jnp.broadcast_to(tile[:, j : j + 1], (8, RANK))

    def row(tile, i):
        return jnp.broadcast_to(tile[i : i + 1, :], (8, RANK))

    col = [{g: lanes(tiles[g], k + j) for g in groups} for j in range(BLOCK)]
    rows = [row(tiles[first], shift + i) for i in range(BLOCK)]
    piv = [[row(col[j][first], shift + i) for j in range(BLOCK)] for i in range(BLOCK)]
    mult = []
    done = []
    pivots = []
    for j in range(BLOCK):
        inverse = 1.0 / piv[j][j]
        pivots.append(piv[j][j])
        done.append(jnp.where(lane == k + j, 1.0, rows[j]))
        for i in range(j + 1, BLOCK):
            factor = piv[i][j] * inverse
            rows[i] = jnp.where(lane == k + j, 0.0, rows[i]) - factor * done[j]
            for m in range(j + 1, BLOCK):
                piv[i][m] = piv[i][m] - factor * piv[j][m]
        mult.append({g: col[j][g] * inverse for g in groups})
        for m in range(j + 1, BLOCK):
            for g in groups:
                col[m][g] = col[m][g] - mult[j][g] * piv[j][m]
    inside = (lane >= k) & (lane < k + BLOCK)
    last = [
        jnp.where((lane > k + j) & (lane < k + BLOCK), 0.0, done[j]) for j in range(BLOCK)
    ]
    for g in groups:
        new = jnp.where(inside, 0.0, tiles[g])
        for j in range(BLOCK):
            new = new - mult[j][g] * last[j]
        if g == first:
            new = jnp.where(sub < shift + BLOCK, tiles[g], new)
            for j in range(BLOCK):
                new = jnp.where(sub == shift + j, done[j], new)
        tiles[g] = new
    return pivots


def factor_steps(t_ref, root_ref, begin, end):
    lane = lax.broadcasted_iota(jnp.int32, (8, RANK), 1)
    sub = lax.broadcasted_iota(jnp.int32, (8, RANK), 0)
    tiles = [t_ref[8 * g : 8 * g + 8, :] for g in range(RANK // 8)]
    for k in range(begin, end, BLOCK):
        pivots = eliminate(tiles, k, lane, sub)
        for j in range(BLOCK):
            root_ref[k + j : k + j + 1, :] = lax.rsqrt(pivots[j])[0:1, :]
    for g in range(RANK // 8):
        t_ref[8 * g : 8 * g + 8, :] = tiles[g]


def make_kernel(hid, r_rows):
    def kernel(
        mom_hbm, grad_hbm, right_hbm,
        out_ref, left_ref, next_ref,
        grad, right_in, right_t, part_sum, total, pairs_t, left_t, acc_r, acc_g,
        from_core, got1, got2, own2, got3,
        r_part, r_core, r_sum, r_y, r_all, t_ref, root_ref, sq_buf, sq_dp,
        load_sem, right_sem, send_sem, recv_sem, r_send, r_recv, sq_send, sq_recv,
    ):
        dp = lax.axis_index("dp")
        mp = lax.axis_index("mp")
        core = lax.rem(dp, 2)
        pos = (lax.rem(mp, 4), dp // 2, mp // 4)
        sibling = device(pos, 1 - core)
        blend = out_ref.at[0]

        def load(i, what):
            src, dst = ((mom_hbm, blend), (grad_hbm, grad))[what]
            return pltpu.make_async_copy(
                src.at[0, :, lanes_at(i * CHUNK, CHUNK)],
                dst.at[:, lanes_at(i * CHUNK, CHUNK)],
                load_sem.at[what, i],
            )

        right_load = pltpu.make_async_copy(right_hbm, right_in, right_sem.at[0])
        right_load.start()
        for i in range(N_CHUNKS):
            load(i, 0).start()
            load(i, 1).start()

        barrier = pltpu.get_barrier_semaphore()
        greet = [sibling]
        greet += [device(moved(pos, a, r), core) for a in range(3) for r in range(1, 4)]
        greet += [device(moved(pos, 1, r), 1 - core) for r in range(1, 4)]
        greet += [
            device(moved(moved(pos, 0, r), 2, s), core) for r in range(1, 4) for s in range(1, 4)
        ]
        for peer in greet:
            pl.semaphore_signal(barrier, inc=1, device_id=peer, device_id_type=MESH)
        right_load.wait()
        right_t[...] = right_in[...].astype(F32).T.astype(BF16)

        def remote(src, dst, send, recv, peer):
            return pltpu.make_async_remote_copy(
                src_ref=src, dst_ref=dst, send_sem=send, recv_sem=recv,
                device_id=peer, device_id_type=MESH,
            )

        def took(ref, sem):
            pltpu.make_async_copy(ref, ref, sem).wait()

        def left_chunks(begin, end):
            def one(i, _):
                load(i, 0).wait()
                load(i, 1).wait()
                at = lanes_at(i * CHUNK, CHUNK)
                value = (blend[:, at].astype(F32) + grad[:, at].astype(F32)).astype(BF16)
                blend[:, at] = value
                terms = jnp.dot(right_t[...], value, preferred_element_type=F32)
                for t in range(CHUNK // 128):
                    rows = rows_at(i * CHUNK + t * 128, 128)
                    part_sum[rows, :] = terms[:, t * 128 : (t + 1) * 128]
                return 0

            lax.fori_loop(begin, end, one, 0)

        def geometry(p):
            begin, chunks, axes = PARTS[p]
            half = chunks * CHUNK // 2
            base = begin * CHUNK
            own = base + core * half
            quarter = half // 4
            small = quarter // 4
            return base, half, own, quarter, small, axes

        def core_send(p):
            base, half, own, quarter, small, axes = geometry(p)
            other = base + (1 - core) * half
            remote(
                part_sum.at[rows_at(other, half)], from_core.at[pl.ds(base // 2, half)],
                send_sem.at[p, 0], recv_sem.at[p, 0], sibling,
            ).start()

        def axis_send(p):
            base, half, own, quarter, small, axes = geometry(p)
            took(from_core.at[pl.ds(base // 2, half)], recv_sem.at[p, 0])
            step = 128
            for r in range(0, half, step):
                size = min(step, half - r)
                part_sum[rows_at(own + r, size), :] += from_core[pl.ds(base // 2 + r, size), :]
            for r in range(1, 4):
                to = lax.rem(pos[axes[0]] + r, 4)
                remote(
                    part_sum.at[rows_at(own + to * quarter, quarter)],
                    got1.at[r - 1, pl.ds(base // 8, quarter)],
                    send_sem.at[p, 1], recv_sem.at[p, 1], device(moved(pos, axes[0], r), core),
                ).start()

        def second_send(p):
            base, half, own, quarter, small, axes = geometry(p)
            here = pl.ds(base // 8, quarter)
            took(got1.at[:, here], recv_sem.at[p, 1])
            mine = rows_at(own + pos[axes[0]] * quarter, quarter)
            got1[0, here, :] = (part_sum[mine, :] + got1[0, here, :]) + (
                got1[1, here, :] + got1[2, here, :]
            )
            for r in range(1, 4):
                to = lax.rem(pos[axes[1]] + r, 4)
                remote(
                    got1.at[0, rows_at(base // 8 + to * small, small)],
                    got2.at[r - 1, pl.ds(base // 32, small)],
                    send_sem.at[p, 2], recv_sem.at[p, 2], device(moved(pos, axes[1], r), core),
                ).start()

        def third_send(p):
            base, half, own, quarter, small, axes = geometry(p)
            here = pl.ds(base // 32, small)
            took(got2.at[:, here], recv_sem.at[p, 2])
            mine = rows_at(base // 8 + pos[axes[1]] * small, small)
            own2[here, :] = (got1[0, mine, :] + got2[0, here, :]) + (
                got2[1, here, :] + got2[2, here, :]
            )
            me = pos[axes[2]]
            for r in range(1, 4):
                remote(
                    own2.at[here],
                    got3.at[r - 1, here],
                    send_sem.at[p, 3], recv_sem.at[p, 3], device(moved(pos, axes[2], r), core),
                ).start()

        def gather_send(p):
            base, half, own, quarter, small, axes = geometry(p)
            here = pl.ds(base // 32, small)
            took(got3.at[:, here], recv_sem.at[p, 3])
            me = pos[axes[2]]
            terms = [own2[here, :]] + [got3[r, here, :] for r in range(3)]

            def at_place(j):
                value = terms[0]
                for r in range(1, 4):
                    value = jnp.where(lax.rem(me + 4 - r, 4) == j, terms[r], value)
                return value

            mine = rows_at(own + pos[axes[0]] * quarter + pos[axes[1]] * small, small)
            total[mine, :] = (at_place(0) + at_place(1)) + (at_place(2) + at_place(3))
            for r in range(1, 4):
                remote(
                    total.at[mine], total.at[mine],
                    send_sem.at[p, 4], recv_sem.at[p, 4], device(moved(pos, axes[1], r), core),
                ).start()

        def gather_axis(p):
            base, half, own, quarter, small, axes = geometry(p)
            took(total.at[pl.ds(0, 3 * small)], recv_sem.at[p, 4])
            mine = rows_at(own + pos[axes[0]] * quarter, quarter)
            for r in range(1, 4):
                remote(
                    total.at[mine], total.at[mine],
                    send_sem.at[p, 5], recv_sem.at[p, 5], device(moved(pos, axes[0], r), core),
                ).start()

        def gather_core(p):
            base, half, own, quarter, small, axes = geometry(p)
            took(total.at[pl.ds(0, 3 * quarter)], recv_sem.at[p, 5])
            mine = rows_at(own, half)
            remote(
                total.at[mine], total.at[mine], send_sem.at[p, 6], recv_sem.at[p, 6], sibling
            ).start()

        def use_half(p, which, first=False):
            base, half, own, quarter, small, axes = geometry(p)
            start = own
            if which:
                took(total.at[pl.ds(0, half)], recv_sem.at[p, 6])
                start = base + (1 - core) * half

            for t in range(half // 128):
                high, low = split(total[rows_at(start + t * 128, 128), :])
                cols = lanes_at(start + t * 128, 128)
                pairs_t[0:RANK, cols] = high
                pairs_t[RANK : 2 * RANK, cols] = low
            cols = lanes_at(start, half)
            terms = pairs_t[:, cols]
            gram = lax.dot_general(terms, terms, NT, preferred_element_type=F32)
            acc_g[...] = gram if first else acc_g[...] + gram
            value = lax.dot_general(blend[:, cols], terms, NT, preferred_element_type=F32)
            acc_r[...] = value if first else acc_r[...] + value

        def sent(p):
            base, half, own, quarter, small, axes = geometry(p)
            took(total.at[pl.ds(0, half)], send_sem.at[p, 0])
            took(total.at[pl.ds(0, 3 * quarter)], send_sem.at[p, 1])
            took(total.at[pl.ds(0, 3 * small)], send_sem.at[p, 2])
            took(total.at[pl.ds(0, 3 * small)], send_sem.at[p, 3])
            took(total.at[pl.ds(0, 3 * small)], send_sem.at[p, 4])
            took(total.at[pl.ds(0, 3 * quarter)], send_sem.at[p, 5])
            took(total.at[pl.ds(0, half)], send_sem.at[p, 6])

        left_chunks(0, 4)
        pl.semaphore_wait(barrier, len(greet))
        core_send(0)
        left_chunks(4, 6)
        axis_send(0)
        left_chunks(6, 7)
        core_send(1)
        left_chunks(7, 9)
        axis_send(1)
        left_chunks(9, 10)
        core_send(2)
        axis_send(2)
        for p in range(3):
            second_send(p)
        for p in range(3):
            third_send(p)
        for p in range(3):
            gather_send(p)
        for p in range(3):
            gather_axis(p)
        gather_core(0)
        gather_core(1)
        use_half(0, 0, first=True)
        use_half(1, 0)
        gather_core(2)
        use_half(0, 1)
        use_half(1, 1)
        use_half(2, 0)
        use_half(2, 1)

        r_part[0:hid, :] = acc_r[:, 0:RANK] + acc_r[:, RANK : 2 * RANK]
        r_part[hid:, :] = jnp.zeros((r_rows - hid, RANK), F32)
        half_rows = r_rows // 2
        remote(
            r_part.at[rows_at((1 - core) * half_rows, half_rows)], r_core,
            r_send.at[0], r_recv.at[0], sibling,
        ).start()
        t_ref[...] = (acc_g[0:RANK, 0:RANK] + acc_g[RANK:, 0:RANK]) + (
            acc_g[0:RANK, RANK:] + acc_g[RANK:, RANK:]
        )
        factor_steps(t_ref, root_ref, 0, 16)
        took(r_core, r_recv.at[0])
        own_half = rows_at(core * half_rows, half_rows)
        r_sum[...] = r_part[own_half, :] + r_core[...]
        piece = half_rows // 4
        for r in range(1, 4):
            to = lax.rem(pos[1] + r, 4)
            remote(
                r_sum.at[rows_at(to * piece, piece)], r_y.at[r - 1],
                r_send.at[1], r_recv.at[1], device(moved(pos, 1, r), core),
            ).start()
        factor_steps(t_ref, root_ref, 16, RANK)
        lane = lax.broadcasted_iota(jnp.int32, (RANK, RANK), 1)
        sub = lax.broadcasted_iota(jnp.int32, (RANK, RANK), 0)
        lower = jnp.where(lane < sub, t_ref[...], jnp.where(lane == sub, 1.0, 0.0)) * root_ref[...]
        took(r_y, r_recv.at[1])
        summed = (r_sum[rows_at(pos[1] * piece, piece), :] + r_y[0]) + (r_y[1] + r_y[2])
        mean = lax.dot_general(
            summed, lower, NT, precision=lax.Precision.HIGHEST, preferred_element_type=F32
        ) * F32(0.125)
        mine = rows_at16(core * half_rows + pos[1] * piece, piece)
        r_all[mine, :] = mean.astype(BF16)
        for r in range(1, 4):
            remote(
                r_all.at[mine], r_all.at[mine],
                r_send.at[2], r_recv.at[2], device(moved(pos, 1, r), core),
            ).start()
        sq_buf[mp] = jnp.broadcast_to(jnp.sum(mean * mean, axis=0, keepdims=True), (8, RANK))
        for s in range(4):
            for r in range(4):
                if r or s:
                    remote(
                        sq_buf.at[mp], sq_buf.at[mp], sq_send.at[0], sq_recv.at[0],
                        device(moved(moved(pos, 0, r), 2, s), core),
                    ).start()

        high, low = split(lower)
        weights = jnp.concatenate(
            [jnp.concatenate([high, high], axis=1), jnp.concatenate([low, low], axis=1)], axis=0
        )
        root = F32(math.sqrt(D))

        for i in range(N_CHUNKS):
            at = slice(i * CHUNK, (i + 1) * CHUNK)
            value = jnp.dot(weights, pairs_t[:, at], preferred_element_type=F32)
            value = (value[:RANK, :] + value[RANK:, :]) * root
            left_t[:, at] = value.astype(BF16)
            left_ref[at, :] = value.T.astype(BF16)
        took(r_all.at[pl.ds(0, 3 * piece)], r_recv.at[2])
        gathered = rows_at16(core * half_rows, half_rows)
        remote(
            r_all.at[gathered], r_all.at[gathered], r_send.at[3], r_recv.at[3], sibling
        ).start()
        took(sq_buf.at[pl.ds(0, 15)], sq_recv.at[0])
        terms = sq_buf[0]
        for i in range(1, 16):
            terms = terms + sq_buf[i]
        sq_dp[dp] = terms
        for r in range(4):
            for c in range(2):
                if r or c:
                    remote(
                        sq_dp.at[dp], sq_dp.at[dp], sq_send.at[1], sq_recv.at[1],
                        device(moved(pos, 1, r), lax.rem(core + c, 2)),
                    ).start()
        took(r_all.at[pl.ds(0, half_rows)], r_recv.at[3])
        coef = F32((1.0 - DECAY) / math.sqrt(D))
        for i in range(N_CHUNKS):
            at = slice(i * CHUNK, (i + 1) * CHUNK)
            low = jnp.dot(r_all[0:hid, :], left_t[:, at], preferred_element_type=F32)
            blend[:, at] = (blend[:, at].astype(F32) - coef * low).astype(BF16)
        took(sq_dp.at[pl.ds(0, 7)], sq_recv.at[1])
        all_squares = sq_dp[0]
        for i in range(1, 8):
            all_squares = all_squares + sq_dp[i]
        scale = jnp.sqrt(all_squares[0:1, :] / (hid * 16) + EPS)
        next_ref[...] = (r_all[0:hid, :].astype(F32) / scale).astype(BF16)

        took(sq_buf.at[pl.ds(0, 15)], sq_send.at[0])
        took(sq_dp.at[pl.ds(0, 7)], sq_send.at[1])
        took(r_y, r_send.at[1])
        took(r_core, r_send.at[0])
        took(r_all.at[pl.ds(0, 3 * piece)], r_send.at[2])
        took(r_all.at[pl.ds(0, half_rows)], r_send.at[3])
        for p in range(3):
            sent(p)

    return kernel


def factors(momentum, gradient, right_factor):
    hid = momentum.shape[1]
    r_rows = -(-hid // 128) * 128
    vmem = pl.BlockSpec(memory_space=pltpu.VMEM)
    hbm = pl.BlockSpec(memory_space=pl.ANY)
    return pl.pallas_call(
        make_kernel(hid, r_rows),
        out_shape=(
            pltpu.VMEM((1, hid, D), BF16),
            pltpu.VMEM((D, RANK), BF16),
            pltpu.VMEM((hid, RANK), BF16),
        ),
        in_specs=[hbm, hbm, pl.BlockSpec(memory_space=pltpu.HBM)],
        out_specs=(vmem, vmem, vmem),
        scratch_shapes=[
            pltpu.VMEM((hid, D), BF16),
            pltpu.VMEM((hid, RANK), BF16),
            pltpu.VMEM((RANK, hid), BF16),
            pltpu.VMEM((D, RANK), F32),
            pltpu.VMEM((D, RANK), F32),
            pltpu.VMEM((2 * RANK, D), BF16),
            pltpu.VMEM((RANK, D), BF16),
            pltpu.VMEM((hid, 2 * RANK), F32),
            pltpu.VMEM((2 * RANK, 2 * RANK), F32),
            pltpu.VMEM((D // 2, RANK), F32),
            pltpu.VMEM((3, D // 8, RANK), F32),
            pltpu.VMEM((3, D // 32, RANK), F32),
            pltpu.VMEM((D // 32, RANK), F32),
            pltpu.VMEM((3, D // 32, RANK), F32),
            pltpu.VMEM((r_rows, RANK), F32),
            pltpu.VMEM((r_rows // 2, RANK), F32),
            pltpu.VMEM((r_rows // 2, RANK), F32),
            pltpu.VMEM((3, r_rows // 8, RANK), F32),
            pltpu.VMEM((r_rows, RANK), BF16),
            pltpu.VMEM((RANK, RANK), F32),
            pltpu.VMEM((RANK, RANK), F32),
            pltpu.VMEM((16, 8, RANK), F32),
            pltpu.VMEM((8, 8, RANK), F32),
            pltpu.SemaphoreType.DMA((2, N_CHUNKS)),
            pltpu.SemaphoreType.DMA((1,)),
            pltpu.SemaphoreType.DMA((3, STAGES)),
            pltpu.SemaphoreType.DMA((3, STAGES)),
            pltpu.SemaphoreType.DMA((4,)),
            pltpu.SemaphoreType.DMA((4,)),
            pltpu.SemaphoreType.DMA((2,)),
            pltpu.SemaphoreType.DMA((2,)),
        ],
        compiler_params=pltpu.CompilerParams(
            collective_id=0, has_side_effects=True, vmem_limit_bytes=40 << 20
        ),
        name="factors",
    )(momentum, gradient, right_factor)


def shards(momentum, gradient, right_factor):
    momentum_next, left_factor, right_next = factors(
        momentum.swapaxes(1, 2),
        gradient.swapaxes(1, 2),
        pltpu.with_memory_space_constraint(right_factor, pltpu.HBM),
    )
    return momentum_next.swapaxes(1, 2), left_factor, right_next


def solution(mesh):
    placed = (P("dp", None, "mp"), P("dp", None, "mp"), P("mp", None))
    return jax.shard_map(
        shards,
        mesh=mesh,
        in_specs=placed,
        out_specs=(P("dp", None, "mp"), P(), P("mp", None)),
        check_vma=False,
    )
```

```python
import functools
import math

import jax
import jax.numpy as jnp
from jax import lax
from jax.experimental import pallas as pl
from jax.experimental.pallas import tpu as pltpu
from jax.sharding import PartitionSpec as P

D = 5120
RANK = 128
DECAY = 0.9
EPS = 1e-06
MESH = pl.DeviceIdType.MESH
F32 = jnp.float32
BF16 = jnp.bfloat16
NT = (((1,), (1,)), ((), ()))

CHUNK = 512
UNIT = 256
N_CHUNKS = D // CHUNK
PARTS = ((0, 7, (0, 1, 2)), (7, 7, (1, 2, 0)), (14, 6, (2, 0, 1)))
STAGES = 7


def device(pos, core):
    return (pos[1] * 2 + core, pos[2] * 4 + pos[0])


def moved(pos, axis, steps):
    at = list(pos)
    at[axis] = lax.rem(pos[axis] + steps, 4)
    return at


def rows_at(start, size):
    return pl.ds(pl.multiple_of(start, 8), size)


def lanes_at(start, size):
    return pl.ds(pl.multiple_of(start, 128), size)


def rows_at16(start, size):
    return pl.ds(pl.multiple_of(start, 16), size)


def split(value):
    high = value.astype(BF16)
    return high, (value - high.astype(F32)).astype(BF16)


BLOCK = 8


def eliminate(tiles, k, lane, sub):
    first, shift = k // 8, k % 8
    groups = range(first, RANK // 8)

    def lanes(tile, j):
        return jnp.broadcast_to(tile[:, j : j + 1], (8, RANK))

    def row(tile, i):
        return jnp.broadcast_to(tile[i : i + 1, :], (8, RANK))

    col = [{g: lanes(tiles[g], k + j) for g in groups} for j in range(BLOCK)]
    rows = [row(tiles[first], shift + i) for i in range(BLOCK)]
    piv = [[row(col[j][first], shift + i) for j in range(BLOCK)] for i in range(BLOCK)]
    mult = []
    done = []
    pivots = []
    for j in range(BLOCK):
        inverse = 1.0 / piv[j][j]
        pivots.append(piv[j][j])
        done.append(jnp.where(lane == k + j, 1.0, rows[j]))
        for i in range(j + 1, BLOCK):
            factor = piv[i][j] * inverse
            rows[i] = jnp.where(lane == k + j, 0.0, rows[i]) - factor * done[j]
            for m in range(j + 1, BLOCK):
                piv[i][m] = piv[i][m] - factor * piv[j][m]
        mult.append({g: col[j][g] * inverse for g in groups})
        for m in range(j + 1, BLOCK):
            for g in groups:
                col[m][g] = col[m][g] - mult[j][g] * piv[j][m]
    inside = (lane >= k) & (lane < k + BLOCK)
    last = [
        jnp.where((lane > k + j) & (lane < k + BLOCK), 0.0, done[j]) for j in range(BLOCK)
    ]
    for g in groups:
        new = jnp.where(inside, 0.0, tiles[g])
        for j in range(BLOCK):
            new = new - mult[j][g] * last[j]
        if g == first:
            new = jnp.where(sub < shift + BLOCK, tiles[g], new)
            for j in range(BLOCK):
                new = jnp.where(sub == shift + j, done[j], new)
        tiles[g] = new
    return pivots


def factor_steps(t_ref, root_ref, begin, end):
    lane = lax.broadcasted_iota(jnp.int32, (8, RANK), 1)
    sub = lax.broadcasted_iota(jnp.int32, (8, RANK), 0)
    tiles = [t_ref[8 * g : 8 * g + 8, :] for g in range(RANK // 8)]
    for k in range(begin, end, BLOCK):
        pivots = eliminate(tiles, k, lane, sub)
        for j in range(BLOCK):
            root_ref[k + j : k + j + 1, :] = lax.rsqrt(pivots[j])[0:1, :]
    for g in range(RANK // 8):
        t_ref[8 * g : 8 * g + 8, :] = tiles[g]


def make_kernel(hid, r_rows):
    def kernel(
        mom_hbm, grad_hbm, right_hbm,
        out_ref, left_ref, next_ref,
        grad, right_in, right_t, part_sum, total, pairs_t, left_t, acc_r, acc_g,
        from_core, got1, got2, own2, got3,
        r_part, r_core, r_sum, r_y, r_all, t_ref, root_ref, sq_buf, sq_dp,
        load_sem, right_sem, send_sem, recv_sem, r_send, r_recv, sq_send, sq_recv,
    ):
        dp = lax.axis_index("dp")
        mp = lax.axis_index("mp")
        core = lax.rem(dp, 2)
        pos = (lax.rem(mp, 4), dp // 2, mp // 4)
        sibling = device(pos, 1 - core)
        blend = out_ref.at[0]

        def load(i, what):
            src, dst = ((mom_hbm, blend), (grad_hbm, grad))[what]
            return pltpu.make_async_copy(
                src.at[0, :, lanes_at(i * CHUNK, CHUNK)],
                dst.at[:, lanes_at(i * CHUNK, CHUNK)],
                load_sem.at[what, i],
            )

        right_load = pltpu.make_async_copy(right_hbm, right_in, right_sem.at[0])
        right_load.start()
        for i in range(N_CHUNKS):
            load(i, 0).start()
            load(i, 1).start()

        barrier = pltpu.get_barrier_semaphore()
        greet = [sibling]
        greet += [device(moved(pos, a, r), core) for a in range(3) for r in range(1, 4)]
        greet += [device(moved(pos, 1, r), 1 - core) for r in range(1, 4)]
        greet += [
            device(moved(moved(pos, 0, r), 2, s), core) for r in range(1, 4) for s in range(1, 4)
        ]
        for peer in greet:
            pl.semaphore_signal(barrier, inc=1, device_id=peer, device_id_type=MESH)
        right_load.wait()
        right_t[...] = right_in[...].astype(F32).T.astype(BF16)

        def remote(src, dst, send, recv, peer):
            return pltpu.make_async_remote_copy(
                src_ref=src, dst_ref=dst, send_sem=send, recv_sem=recv,
                device_id=peer, device_id_type=MESH,
            )

        def took(ref, sem):
            pltpu.make_async_copy(ref, ref, sem).wait()

        def left_chunks(begin, end):
            def one(i, _):
                load(i, 0).wait()
                load(i, 1).wait()
                at = lanes_at(i * CHUNK, CHUNK)
                value = (blend[:, at].astype(F32) + grad[:, at].astype(F32)).astype(BF16)
                blend[:, at] = value
                terms = jnp.dot(right_t[...], value, preferred_element_type=F32)
                for t in range(CHUNK // 128):
                    rows = rows_at(i * CHUNK + t * 128, 128)
                    part_sum[rows, :] = terms[:, t * 128 : (t + 1) * 128]
                return 0

            lax.fori_loop(begin, end, one, 0)

        def geometry(p):
            begin, units, axes = PARTS[p]
            half = units * UNIT // 2
            base = begin * UNIT
            own = base + core * half
            quarter = half // 4
            small = quarter // 4
            return base, half, own, quarter, small, axes

        def core_send(p):
            base, half, own, quarter, small, axes = geometry(p)
            other = base + (1 - core) * half
            remote(
                part_sum.at[rows_at(other, half)], from_core.at[pl.ds(base // 2, half)],
                send_sem.at[p, 0], recv_sem.at[p, 0], sibling,
            ).start()

        def axis_send(p):
            base, half, own, quarter, small, axes = geometry(p)
            took(from_core.at[pl.ds(base // 2, half)], recv_sem.at[p, 0])
            step = 128
            for r in range(0, half, step):
                size = min(step, half - r)
                part_sum[rows_at(own + r, size), :] += from_core[pl.ds(base // 2 + r, size), :]
            for r in range(1, 4):
                to = lax.rem(pos[axes[0]] + r, 4)
                remote(
                    part_sum.at[rows_at(own + to * quarter, quarter)],
                    got1.at[r - 1, pl.ds(base // 8, quarter)],
                    send_sem.at[p, 1], recv_sem.at[p, 1], device(moved(pos, axes[0], r), core),
                ).start()

        def second_send(p):
            base, half, own, quarter, small, axes = geometry(p)
            here = pl.ds(base // 8, quarter)
            took(got1.at[:, here], recv_sem.at[p, 1])
            mine = rows_at(own + pos[axes[0]] * quarter, quarter)
            got1[0, here, :] = (part_sum[mine, :] + got1[0, here, :]) + (
                got1[1, here, :] + got1[2, here, :]
            )
            for r in range(1, 4):
                to = lax.rem(pos[axes[1]] + r, 4)
                remote(
                    got1.at[0, rows_at(base // 8 + to * small, small)],
                    got2.at[r - 1, pl.ds(base // 32, small)],
                    send_sem.at[p, 2], recv_sem.at[p, 2], device(moved(pos, axes[1], r), core),
                ).start()

        def third_send(p):
            base, half, own, quarter, small, axes = geometry(p)
            here = pl.ds(base // 32, small)
            took(got2.at[:, here], recv_sem.at[p, 2])
            mine = rows_at(base // 8 + pos[axes[1]] * small, small)
            own2[here, :] = (got1[0, mine, :] + got2[0, here, :]) + (
                got2[1, here, :] + got2[2, here, :]
            )
            me = pos[axes[2]]
            for r in range(1, 4):
                remote(
                    own2.at[here],
                    got3.at[r - 1, here],
                    send_sem.at[p, 3], recv_sem.at[p, 3], device(moved(pos, axes[2], r), core),
                ).start()

        def gather_send(p):
            base, half, own, quarter, small, axes = geometry(p)
            here = pl.ds(base // 32, small)
            took(got3.at[:, here], recv_sem.at[p, 3])
            me = pos[axes[2]]
            terms = [own2[here, :]] + [got3[r, here, :] for r in range(3)]

            def at_place(j):
                value = terms[0]
                for r in range(1, 4):
                    value = jnp.where(lax.rem(me + 4 - r, 4) == j, terms[r], value)
                return value

            mine = rows_at(own + pos[axes[0]] * quarter + pos[axes[1]] * small, small)
            total[mine, :] = (at_place(0) + at_place(1)) + (at_place(2) + at_place(3))
            for r in range(1, 4):
                remote(
                    total.at[mine], total.at[mine],
                    send_sem.at[p, 4], recv_sem.at[p, 4], device(moved(pos, axes[1], r), core),
                ).start()

        def gather_axis(p):
            base, half, own, quarter, small, axes = geometry(p)
            took(total.at[pl.ds(0, 3 * small)], recv_sem.at[p, 4])
            mine = rows_at(own + pos[axes[0]] * quarter, quarter)
            for r in range(1, 4):
                remote(
                    total.at[mine], total.at[mine],
                    send_sem.at[p, 5], recv_sem.at[p, 5], device(moved(pos, axes[0], r), core),
                ).start()

        def gather_core(p):
            base, half, own, quarter, small, axes = geometry(p)
            took(total.at[pl.ds(0, 3 * quarter)], recv_sem.at[p, 5])
            mine = rows_at(own, half)
            remote(
                total.at[mine], total.at[mine], send_sem.at[p, 6], recv_sem.at[p, 6], sibling
            ).start()

        def use_half(p, which, first=False):
            base, half, own, quarter, small, axes = geometry(p)
            start = own
            if which:
                took(total.at[pl.ds(0, half)], recv_sem.at[p, 6])
                start = base + (1 - core) * half

            for t in range(half // 128):
                high, low = split(total[rows_at(start + t * 128, 128), :])
                cols = lanes_at(start + t * 128, 128)
                pairs_t[0:RANK, cols] = high
                pairs_t[RANK : 2 * RANK, cols] = low
            cols = lanes_at(start, half)
            terms = pairs_t[:, cols]
            gram = lax.dot_general(terms, terms, NT, preferred_element_type=F32)
            acc_g[...] = gram if first else acc_g[...] + gram
            value = lax.dot_general(blend[:, cols], terms, NT, preferred_element_type=F32)
            acc_r[...] = value if first else acc_r[...] + value

        def sent(p):
            base, half, own, quarter, small, axes = geometry(p)
            took(total.at[pl.ds(0, half)], send_sem.at[p, 0])
            took(total.at[pl.ds(0, 3 * quarter)], send_sem.at[p, 1])
            took(total.at[pl.ds(0, 3 * small)], send_sem.at[p, 2])
            took(total.at[pl.ds(0, 3 * small)], send_sem.at[p, 3])
            took(total.at[pl.ds(0, 3 * small)], send_sem.at[p, 4])
            took(total.at[pl.ds(0, 3 * quarter)], send_sem.at[p, 5])
            took(total.at[pl.ds(0, half)], send_sem.at[p, 6])

        left_chunks(0, 4)
        pl.semaphore_wait(barrier, len(greet))
        core_send(0)
        left_chunks(4, 6)
        axis_send(0)
        left_chunks(6, 7)
        core_send(1)
        left_chunks(7, 9)
        axis_send(1)
        left_chunks(9, 10)
        core_send(2)
        axis_send(2)
        for p in range(3):
            second_send(p)
        for p in range(3):
            third_send(p)
        for p in range(3):
            gather_send(p)
        for p in range(3):
            gather_axis(p)
        gather_core(0)
        gather_core(1)
        use_half(0, 0, first=True)
        use_half(1, 0)
        gather_core(2)
        use_half(0, 1)
        use_half(1, 1)
        use_half(2, 0)
        use_half(2, 1)

        r_part[0:hid, :] = acc_r[:, 0:RANK] + acc_r[:, RANK : 2 * RANK]
        r_part[hid:, :] = jnp.zeros((r_rows - hid, RANK), F32)
        half_rows = r_rows // 2
        remote(
            r_part.at[rows_at((1 - core) * half_rows, half_rows)], r_core,
            r_send.at[0], r_recv.at[0], sibling,
        ).start()
        t_ref[...] = (acc_g[0:RANK, 0:RANK] + acc_g[RANK:, 0:RANK]) + (
            acc_g[0:RANK, RANK:] + acc_g[RANK:, RANK:]
        )
        factor_steps(t_ref, root_ref, 0, 16)
        took(r_core, r_recv.at[0])
        own_half = rows_at(core * half_rows, half_rows)
        r_sum[...] = r_part[own_half, :] + r_core[...]
        piece = half_rows // 4
        for r in range(1, 4):
            to = lax.rem(pos[1] + r, 4)
            remote(
                r_sum.at[rows_at(to * piece, piece)], r_y.at[r - 1],
                r_send.at[1], r_recv.at[1], device(moved(pos, 1, r), core),
            ).start()
        factor_steps(t_ref, root_ref, 16, RANK)
        lane = lax.broadcasted_iota(jnp.int32, (RANK, RANK), 1)
        sub = lax.broadcasted_iota(jnp.int32, (RANK, RANK), 0)
        lower = jnp.where(lane < sub, t_ref[...], jnp.where(lane == sub, 1.0, 0.0)) * root_ref[...]
        took(r_y, r_recv.at[1])
        summed = (r_sum[rows_at(pos[1] * piece, piece), :] + r_y[0]) + (r_y[1] + r_y[2])
        mean = lax.dot_general(
            summed, lower, NT, precision=lax.Precision.HIGHEST, preferred_element_type=F32
        ) * F32(0.125)
        mine = rows_at16(core * half_rows + pos[1] * piece, piece)
        r_all[mine, :] = mean.astype(BF16)
        for r in range(1, 4):
            remote(
                r_all.at[mine], r_all.at[mine],
                r_send.at[2], r_recv.at[2], device(moved(pos, 1, r), core),
            ).start()
        sq_buf[mp] = jnp.broadcast_to(jnp.sum(mean * mean, axis=0, keepdims=True), (8, RANK))
        for s in range(4):
            for r in range(4):
                if r or s:
                    remote(
                        sq_buf.at[mp], sq_buf.at[mp], sq_send.at[0], sq_recv.at[0],
                        device(moved(moved(pos, 0, r), 2, s), core),
                    ).start()

        high, low = split(lower)
        weights = jnp.concatenate(
            [jnp.concatenate([high, high], axis=1), jnp.concatenate([low, low], axis=1)], axis=0
        )
        root = F32(math.sqrt(D))

        for i in range(N_CHUNKS):
            at = slice(i * CHUNK, (i + 1) * CHUNK)
            value = jnp.dot(weights, pairs_t[:, at], preferred_element_type=F32)
            value = (value[:RANK, :] + value[RANK:, :]) * root
            left_t[:, at] = value.astype(BF16)
            left_ref[at, :] = value.T.astype(BF16)
        took(r_all.at[pl.ds(0, 3 * piece)], r_recv.at[2])
        gathered = rows_at16(core * half_rows, half_rows)
        remote(
            r_all.at[gathered], r_all.at[gathered], r_send.at[3], r_recv.at[3], sibling
        ).start()
        took(sq_buf.at[pl.ds(0, 15)], sq_recv.at[0])
        terms = sq_buf[0]
        for i in range(1, 16):
            terms = terms + sq_buf[i]
        sq_dp[dp] = terms
        for r in range(4):
            for c in range(2):
                if r or c:
                    remote(
                        sq_dp.at[dp], sq_dp.at[dp], sq_send.at[1], sq_recv.at[1],
                        device(moved(pos, 1, r), lax.rem(core + c, 2)),
                    ).start()
        took(r_all.at[pl.ds(0, half_rows)], r_recv.at[3])
        coef = F32((1.0 - DECAY) / math.sqrt(D))
        for i in range(N_CHUNKS):
            at = slice(i * CHUNK, (i + 1) * CHUNK)
            low = jnp.dot(r_all[0:hid, :], left_t[:, at], preferred_element_type=F32)
            blend[:, at] = (blend[:, at].astype(F32) - coef * low).astype(BF16)
        took(sq_dp.at[pl.ds(0, 7)], sq_recv.at[1])
        all_squares = sq_dp[0]
        for i in range(1, 8):
            all_squares = all_squares + sq_dp[i]
        scale = jnp.sqrt(all_squares[0:1, :] / (hid * 16) + EPS)
        next_ref[...] = (r_all[0:hid, :].astype(F32) / scale).astype(BF16)

        took(sq_buf.at[pl.ds(0, 15)], sq_send.at[0])
        took(sq_dp.at[pl.ds(0, 7)], sq_send.at[1])
        took(r_y, r_send.at[1])
        took(r_core, r_send.at[0])
        took(r_all.at[pl.ds(0, 3 * piece)], r_send.at[2])
        took(r_all.at[pl.ds(0, half_rows)], r_send.at[3])
        for p in range(3):
            sent(p)

    return kernel


def factors(momentum, gradient, right_factor):
    hid = momentum.shape[1]
    r_rows = -(-hid // 128) * 128
    vmem = pl.BlockSpec(memory_space=pltpu.VMEM)
    hbm = pl.BlockSpec(memory_space=pl.ANY)
    return pl.pallas_call(
        make_kernel(hid, r_rows),
        out_shape=(
            pltpu.VMEM((1, hid, D), BF16),
            pltpu.VMEM((D, RANK), BF16),
            pltpu.VMEM((hid, RANK), BF16),
        ),
        in_specs=[hbm, hbm, pl.BlockSpec(memory_space=pltpu.HBM)],
        out_specs=(vmem, vmem, vmem),
        scratch_shapes=[
            pltpu.VMEM((hid, D), BF16),
            pltpu.VMEM((hid, RANK), BF16),
            pltpu.VMEM((RANK, hid), BF16),
            pltpu.VMEM((D, RANK), F32),
            pltpu.VMEM((D, RANK), F32),
            pltpu.VMEM((2 * RANK, D), BF16),
            pltpu.VMEM((RANK, D), BF16),
            pltpu.VMEM((hid, 2 * RANK), F32),
            pltpu.VMEM((2 * RANK, 2 * RANK), F32),
            pltpu.VMEM((D // 2, RANK), F32),
            pltpu.VMEM((3, D // 8, RANK), F32),
            pltpu.VMEM((3, D // 32, RANK), F32),
            pltpu.VMEM((D // 32, RANK), F32),
            pltpu.VMEM((3, D // 32, RANK), F32),
            pltpu.VMEM((r_rows, RANK), F32),
            pltpu.VMEM((r_rows // 2, RANK), F32),
            pltpu.VMEM((r_rows // 2, RANK), F32),
            pltpu.VMEM((3, r_rows // 8, RANK), F32),
            pltpu.VMEM((r_rows, RANK), BF16),
            pltpu.VMEM((RANK, RANK), F32),
            pltpu.VMEM((RANK, RANK), F32),
            pltpu.VMEM((16, 8, RANK), F32),
            pltpu.VMEM((8, 8, RANK), F32),
            pltpu.SemaphoreType.DMA((2, N_CHUNKS)),
            pltpu.SemaphoreType.DMA((1,)),
            pltpu.SemaphoreType.DMA((3, STAGES)),
            pltpu.SemaphoreType.DMA((3, STAGES)),
            pltpu.SemaphoreType.DMA((4,)),
            pltpu.SemaphoreType.DMA((4,)),
            pltpu.SemaphoreType.DMA((2,)),
            pltpu.SemaphoreType.DMA((2,)),
        ],
        compiler_params=pltpu.CompilerParams(
            collective_id=0, has_side_effects=True, vmem_limit_bytes=40 << 20
        ),
        name="factors",
    )(momentum, gradient, right_factor)


def store_kernel(momentum_ref, left_ref, next_ref, momentum_hbm, left_hbm, next_hbm, sem):
    rows = momentum_ref.shape[1] // 5
    copies = [
        pltpu.make_async_copy(
            momentum_ref.at[0, i * rows : (i + 1) * rows],
            momentum_hbm.at[0, i * rows : (i + 1) * rows],
            sem.at[i],
        )
        for i in range(5)
    ]
    copies.append(pltpu.make_async_copy(left_ref, left_hbm, sem.at[5]))
    copies.append(pltpu.make_async_copy(next_ref, next_hbm, sem.at[6]))
    for copy in copies:
        copy.start()
    for copy in copies:
        copy.wait()


def store(*outputs):
    vmem = pl.BlockSpec(memory_space=pltpu.VMEM)
    hbm = pl.BlockSpec(memory_space=pltpu.HBM)
    return pl.pallas_call(
        store_kernel,
        out_shape=tuple(jax.ShapeDtypeStruct(x.shape, x.dtype) for x in outputs),
        in_specs=[vmem] * 3,
        out_specs=(hbm,) * 3,
        scratch_shapes=[pltpu.SemaphoreType.DMA((7,))],
        compiler_params=pltpu.CompilerParams(vmem_limit_bytes=4 << 20),
        name="store",
    )(*(pltpu.with_memory_space_constraint(x, pltpu.VMEM) for x in outputs))


def shards(momentum, gradient, right_factor):
    outputs = factors(
        momentum.swapaxes(1, 2),
        gradient.swapaxes(1, 2),
        pltpu.with_memory_space_constraint(right_factor, pltpu.HBM),
    )
    momentum_next, left_factor, right_next = store(*outputs)
    return momentum_next.swapaxes(1, 2), left_factor, right_next


def solution(mesh):
    placed = (P("dp", None, "mp"), P("dp", None, "mp"), P("mp", None))
    return jax.shard_map(
        shards,
        mesh=mesh,
        in_specs=placed,
        out_specs=(P("dp", None, "mp"), P(), P("mp", None)),
        check_vma=False,
    )
```

```python
import functools
import math

import jax
import jax.numpy as jnp
from jax import lax
from jax.experimental import pallas as pl
from jax.experimental.pallas import tpu as pltpu
from jax.sharding import PartitionSpec as P

D = 5120
RANK = 128
DECAY = 0.9
EPS = 1e-06
MESH = pl.DeviceIdType.MESH
F32 = jnp.float32
BF16 = jnp.bfloat16
NT = (((1,), (1,)), ((), ()))

CHUNK = 512
UNIT = 256
N_CHUNKS = D // CHUNK
PARTS = ((0, 7, (0, 1, 2)), (7, 7, (1, 2, 0)), (14, 6, (2, 0, 1)))
STAGES = 7


def device(pos, core):
    return (pos[1] * 2 + core, pos[2] * 4 + pos[0])


def moved(pos, axis, steps):
    at = list(pos)
    at[axis] = lax.rem(pos[axis] + steps, 4)
    return at


def rows_at(start, size):
    return pl.ds(pl.multiple_of(start, 8), size)


def lanes_at(start, size):
    return pl.ds(pl.multiple_of(start, 128), size)


def rows_at16(start, size):
    return pl.ds(pl.multiple_of(start, 16), size)


def split(value):
    high = value.astype(BF16)
    return high, (value - high.astype(F32)).astype(BF16)


BLOCK = 8


def eliminate(tiles, k, lane, sub):
    first, shift = k // 8, k % 8
    groups = range(first, RANK // 8)

    def lanes(tile, j):
        return jnp.broadcast_to(tile[:, j : j + 1], (8, RANK))

    def row(tile, i):
        return jnp.broadcast_to(tile[i : i + 1, :], (8, RANK))

    col = [{g: lanes(tiles[g], k + j) for g in groups} for j in range(BLOCK)]
    rows = [row(tiles[first], shift + i) for i in range(BLOCK)]
    piv = [[row(col[j][first], shift + i) for j in range(BLOCK)] for i in range(BLOCK)]
    mult = []
    done = []
    pivots = []
    for j in range(BLOCK):
        inverse = 1.0 / piv[j][j]
        pivots.append(piv[j][j])
        done.append(jnp.where(lane == k + j, 1.0, rows[j]))
        for i in range(j + 1, BLOCK):
            factor = piv[i][j] * inverse
            rows[i] = jnp.where(lane == k + j, 0.0, rows[i]) - factor * done[j]
            for m in range(j + 1, BLOCK):
                piv[i][m] = piv[i][m] - factor * piv[j][m]
        mult.append({g: col[j][g] * inverse for g in groups})
        for m in range(j + 1, BLOCK):
            for g in groups:
                col[m][g] = col[m][g] - mult[j][g] * piv[j][m]
    inside = (lane >= k) & (lane < k + BLOCK)
    last = [
        jnp.where((lane > k + j) & (lane < k + BLOCK), 0.0, done[j]) for j in range(BLOCK)
    ]
    for g in groups:
        new = jnp.where(inside, 0.0, tiles[g])
        for j in range(BLOCK):
            new = new - mult[j][g] * last[j]
        if g == first:
            new = jnp.where(sub < shift + BLOCK, tiles[g], new)
            for j in range(BLOCK):
                new = jnp.where(sub == shift + j, done[j], new)
        tiles[g] = new
    return pivots


def factor_steps(t_ref, root_ref, begin, end):
    lane = lax.broadcasted_iota(jnp.int32, (8, RANK), 1)
    sub = lax.broadcasted_iota(jnp.int32, (8, RANK), 0)
    tiles = [t_ref[8 * g : 8 * g + 8, :] for g in range(RANK // 8)]
    for k in range(begin, end, BLOCK):
        pivots = eliminate(tiles, k, lane, sub)
        for j in range(BLOCK):
            root_ref[k + j : k + j + 1, :] = lax.rsqrt(pivots[j])[0:1, :]
    for g in range(RANK // 8):
        t_ref[8 * g : 8 * g + 8, :] = tiles[g]


def make_kernel(hid, r_rows):
    def kernel(
        mom_hbm, grad_hbm, right_hbm,
        out_ref, left_ref, next_ref,
        grad, right_in, right_t, part_sum, total, pairs_t, left_t, acc_r, acc_g,
        from_core, got1, got2, own2, got3,
        r_part, r_core, r_sum, r_y, r_all, t_ref, root_ref, sq_buf, sq_dp,
        load_sem, right_sem, send_sem, recv_sem, r_send, r_recv, sq_send, sq_recv,
    ):
        dp = lax.axis_index("dp")
        mp = lax.axis_index("mp")
        core = lax.rem(dp, 2)
        pos = (lax.rem(mp, 4), dp // 2, mp // 4)
        sibling = device(pos, 1 - core)
        blend = out_ref.at[0]

        def load(i, what):
            src, dst = ((mom_hbm, blend), (grad_hbm, grad))[what]
            return pltpu.make_async_copy(
                src.at[0, :, lanes_at(i * CHUNK, CHUNK)],
                dst.at[:, lanes_at(i * CHUNK, CHUNK)],
                load_sem.at[what, i],
            )

        right_load = pltpu.make_async_copy(right_hbm, right_in, right_sem.at[0])
        right_load.start()
        for i in range(N_CHUNKS):
            load(i, 0).start()
            load(i, 1).start()

        barrier = pltpu.get_barrier_semaphore()
        greet = [sibling]
        greet += [device(moved(pos, a, r), core) for a in range(3) for r in range(1, 4)]
        greet += [device(moved(pos, 1, r), 1 - core) for r in range(1, 4)]
        greet += [
            device(moved(moved(pos, 0, r), 2, s), core) for r in range(1, 4) for s in range(1, 4)
        ]
        for peer in greet:
            pl.semaphore_signal(barrier, inc=1, device_id=peer, device_id_type=MESH)
        right_load.wait()
        right_t[...] = right_in[...].astype(F32).T.astype(BF16)

        def remote(src, dst, send, recv, peer):
            return pltpu.make_async_remote_copy(
                src_ref=src, dst_ref=dst, send_sem=send, recv_sem=recv,
                device_id=peer, device_id_type=MESH,
            )

        def took(ref, sem):
            pltpu.make_async_copy(ref, ref, sem).wait()

        def left_chunks(begin, end):
            def one(i, _):
                load(i, 0).wait()
                load(i, 1).wait()
                at = lanes_at(i * CHUNK, CHUNK)
                value = (blend[:, at].astype(F32) + grad[:, at].astype(F32)).astype(BF16)
                blend[:, at] = value
                terms = jnp.dot(right_t[...], value, preferred_element_type=F32)
                for t in range(CHUNK // 128):
                    rows = rows_at(i * CHUNK + t * 128, 128)
                    part_sum[rows, :] = terms[:, t * 128 : (t + 1) * 128]
                return 0

            lax.fori_loop(begin, end, one, 0)

        def geometry(p):
            begin, units, axes = PARTS[p]
            half = units * UNIT // 2
            base = begin * UNIT
            own = base + core * half
            quarter = half // 4
            small = quarter // 4
            return base, half, own, quarter, small, axes

        def core_send(p):
            base, half, own, quarter, small, axes = geometry(p)
            other = base + (1 - core) * half
            remote(
                part_sum.at[rows_at(other, half)], from_core.at[pl.ds(base // 2, half)],
                send_sem.at[p, 0], recv_sem.at[p, 0], sibling,
            ).start()

        def axis_send(p):
            base, half, own, quarter, small, axes = geometry(p)
            took(from_core.at[pl.ds(base // 2, half)], recv_sem.at[p, 0])
            step = 128
            for r in range(0, half, step):
                size = min(step, half - r)
                part_sum[rows_at(own + r, size), :] += from_core[pl.ds(base // 2 + r, size), :]
            for r in range(1, 4):
                to = lax.rem(pos[axes[0]] + r, 4)
                remote(
                    part_sum.at[rows_at(own + to * quarter, quarter)],
                    got1.at[r - 1, pl.ds(base // 8, quarter)],
                    send_sem.at[p, 1], recv_sem.at[p, 1], device(moved(pos, axes[0], r), core),
                ).start()

        def second_send(p):
            base, half, own, quarter, small, axes = geometry(p)
            here = pl.ds(base // 8, quarter)
            took(got1.at[:, here], recv_sem.at[p, 1])
            mine = rows_at(own + pos[axes[0]] * quarter, quarter)
            got1[0, here, :] = (part_sum[mine, :] + got1[0, here, :]) + (
                got1[1, here, :] + got1[2, here, :]
            )
            for r in range(1, 4):
                to = lax.rem(pos[axes[1]] + r, 4)
                remote(
                    got1.at[0, rows_at(base // 8 + to * small, small)],
                    got2.at[r - 1, pl.ds(base // 32, small)],
                    send_sem.at[p, 2], recv_sem.at[p, 2], device(moved(pos, axes[1], r), core),
                ).start()

        def third_send(p):
            base, half, own, quarter, small, axes = geometry(p)
            here = pl.ds(base // 32, small)
            took(got2.at[:, here], recv_sem.at[p, 2])
            mine = rows_at(base // 8 + pos[axes[1]] * small, small)
            own2[here, :] = (got1[0, mine, :] + got2[0, here, :]) + (
                got2[1, here, :] + got2[2, here, :]
            )
            me = pos[axes[2]]
            for r in range(1, 4):
                remote(
                    own2.at[here],
                    got3.at[r - 1, here],
                    send_sem.at[p, 3], recv_sem.at[p, 3], device(moved(pos, axes[2], r), core),
                ).start()

        def gather_send(p):
            base, half, own, quarter, small, axes = geometry(p)
            here = pl.ds(base // 32, small)
            took(got3.at[:, here], recv_sem.at[p, 3])
            me = pos[axes[2]]
            terms = [own2[here, :]] + [got3[r, here, :] for r in range(3)]

            def at_place(j):
                value = terms[0]
                for r in range(1, 4):
                    value = jnp.where(lax.rem(me + 4 - r, 4) == j, terms[r], value)
                return value

            mine = rows_at(own + pos[axes[0]] * quarter + pos[axes[1]] * small, small)
            total[mine, :] = (at_place(0) + at_place(1)) + (at_place(2) + at_place(3))
            for r in range(1, 4):
                remote(
                    total.at[mine], total.at[mine],
                    send_sem.at[p, 4], recv_sem.at[p, 4], device(moved(pos, axes[1], r), core),
                ).start()

        def gather_axis(p):
            base, half, own, quarter, small, axes = geometry(p)
            took(total.at[pl.ds(0, 3 * small)], recv_sem.at[p, 4])
            mine = rows_at(own + pos[axes[0]] * quarter, quarter)
            for r in range(1, 4):
                remote(
                    total.at[mine], total.at[mine],
                    send_sem.at[p, 5], recv_sem.at[p, 5], device(moved(pos, axes[0], r), core),
                ).start()

        def gather_core(p):
            base, half, own, quarter, small, axes = geometry(p)
            took(total.at[pl.ds(0, 3 * quarter)], recv_sem.at[p, 5])
            mine = rows_at(own, half)
            remote(
                total.at[mine], total.at[mine], send_sem.at[p, 6], recv_sem.at[p, 6], sibling
            ).start()

        def use_half(p, which, first=False):
            base, half, own, quarter, small, axes = geometry(p)
            start = own
            if which:
                took(total.at[pl.ds(0, half)], recv_sem.at[p, 6])
                start = base + (1 - core) * half

            for t in range(half // 128):
                high, low = split(total[rows_at(start + t * 128, 128), :])
                cols = lanes_at(start + t * 128, 128)
                pairs_t[0:RANK, cols] = high
                pairs_t[RANK : 2 * RANK, cols] = low
            cols = lanes_at(start, half)
            terms = pairs_t[:, cols]
            gram = lax.dot_general(terms, terms, NT, preferred_element_type=F32)
            acc_g[...] = gram if first else acc_g[...] + gram
            value = lax.dot_general(blend[:, cols], terms, NT, preferred_element_type=F32)
            acc_r[...] = value if first else acc_r[...] + value

        def sent(p):
            base, half, own, quarter, small, axes = geometry(p)
            took(total.at[pl.ds(0, half)], send_sem.at[p, 0])
            took(total.at[pl.ds(0, 3 * quarter)], send_sem.at[p, 1])
            took(total.at[pl.ds(0, 3 * small)], send_sem.at[p, 2])
            took(total.at[pl.ds(0, 3 * small)], send_sem.at[p, 3])
            took(total.at[pl.ds(0, 3 * small)], send_sem.at[p, 4])
            took(total.at[pl.ds(0, 3 * quarter)], send_sem.at[p, 5])
            took(total.at[pl.ds(0, half)], send_sem.at[p, 6])

        left_chunks(0, 4)
        pl.semaphore_wait(barrier, len(greet))
        core_send(0)
        left_chunks(4, 6)
        axis_send(0)
        left_chunks(6, 7)
        core_send(1)
        left_chunks(7, 9)
        axis_send(1)
        left_chunks(9, 10)
        core_send(2)
        axis_send(2)
        for p in range(3):
            second_send(p)
        for p in range(3):
            third_send(p)
        for p in range(3):
            gather_send(p)
        for p in range(3):
            gather_axis(p)
        gather_core(0)
        gather_core(1)
        use_half(0, 0, first=True)
        use_half(1, 0)
        gather_core(2)
        use_half(0, 1)
        use_half(1, 1)
        use_half(2, 0)
        use_half(2, 1)

        r_part[0:hid, :] = acc_r[:, 0:RANK] + acc_r[:, RANK : 2 * RANK]
        r_part[hid:, :] = jnp.zeros((r_rows - hid, RANK), F32)
        half_rows = r_rows // 2
        remote(
            r_part.at[rows_at((1 - core) * half_rows, half_rows)], r_core,
            r_send.at[0], r_recv.at[0], sibling,
        ).start()
        t_ref[...] = (acc_g[0:RANK, 0:RANK] + acc_g[RANK:, 0:RANK]) + (
            acc_g[0:RANK, RANK:] + acc_g[RANK:, RANK:]
        )
        factor_steps(t_ref, root_ref, 0, 16)
        took(r_core, r_recv.at[0])
        own_half = rows_at(core * half_rows, half_rows)
        r_sum[...] = r_part[own_half, :] + r_core[...]
        piece = half_rows // 4
        for r in range(1, 4):
            to = lax.rem(pos[1] + r, 4)
            remote(
                r_sum.at[rows_at(to * piece, piece)], r_y.at[r - 1],
                r_send.at[1], r_recv.at[1], device(moved(pos, 1, r), core),
            ).start()
        factor_steps(t_ref, root_ref, 16, RANK)
        lane = lax.broadcasted_iota(jnp.int32, (RANK, RANK), 1)
        sub = lax.broadcasted_iota(jnp.int32, (RANK, RANK), 0)
        lower = jnp.where(lane < sub, t_ref[...], jnp.where(lane == sub, 1.0, 0.0)) * root_ref[...]
        took(r_y, r_recv.at[1])
        summed = (r_sum[rows_at(pos[1] * piece, piece), :] + r_y[0]) + (r_y[1] + r_y[2])
        mean = lax.dot_general(
            summed, lower, NT, precision=lax.Precision.HIGHEST, preferred_element_type=F32
        ) * F32(0.125)
        mine = rows_at16(core * half_rows + pos[1] * piece, piece)
        r_all[mine, :] = mean.astype(BF16)
        sq_buf[mp] = jnp.broadcast_to(jnp.sum(mean * mean, axis=0, keepdims=True), (8, RANK))
        for s in range(4):
            for r in range(4):
                if r or s:
                    remote(
                        sq_buf.at[mp], sq_buf.at[mp], sq_send.at[0], sq_recv.at[0],
                        device(moved(moved(pos, 0, r), 2, s), core),
                    ).start()
        for r in range(1, 4):
            remote(
                r_all.at[mine], r_all.at[mine],
                r_send.at[2], r_recv.at[2], device(moved(pos, 1, r), core),
            ).start()

        high, low = split(lower)
        weights = jnp.concatenate(
            [jnp.concatenate([high, high], axis=1), jnp.concatenate([low, low], axis=1)], axis=0
        )
        root = F32(math.sqrt(D))

        for i in range(N_CHUNKS):
            at = slice(i * CHUNK, (i + 1) * CHUNK)
            value = jnp.dot(weights, pairs_t[:, at], preferred_element_type=F32)
            value = (value[:RANK, :] + value[RANK:, :]) * root
            left_t[:, at] = value.astype(BF16)
            left_ref[at, :] = value.T.astype(BF16)
        took(r_all.at[pl.ds(0, 3 * piece)], r_recv.at[2])
        gathered = rows_at16(core * half_rows, half_rows)
        remote(
            r_all.at[gathered], r_all.at[gathered], r_send.at[3], r_recv.at[3], sibling
        ).start()
        took(sq_buf.at[pl.ds(0, 15)], sq_recv.at[0])
        terms = sq_buf[0]
        for i in range(1, 16):
            terms = terms + sq_buf[i]
        sq_dp[dp] = terms
        for r in range(4):
            for c in range(2):
                if r or c:
                    remote(
                        sq_dp.at[dp], sq_dp.at[dp], sq_send.at[1], sq_recv.at[1],
                        device(moved(pos, 1, r), lax.rem(core + c, 2)),
                    ).start()
        took(r_all.at[pl.ds(0, half_rows)], r_recv.at[3])
        coef = F32((1.0 - DECAY) / math.sqrt(D))
        for i in range(N_CHUNKS):
            at = slice(i * CHUNK, (i + 1) * CHUNK)
            low = jnp.dot(r_all[0:hid, :], left_t[:, at], preferred_element_type=F32)
            blend[:, at] = (blend[:, at].astype(F32) - coef * low).astype(BF16)
        took(sq_dp.at[pl.ds(0, 7)], sq_recv.at[1])
        all_squares = sq_dp[0]
        for i in range(1, 8):
            all_squares = all_squares + sq_dp[i]
        scale = jnp.sqrt(all_squares[0:1, :] / (hid * 16) + EPS)
        next_ref[...] = (r_all[0:hid, :].astype(F32) / scale).astype(BF16)

        took(sq_buf.at[pl.ds(0, 15)], sq_send.at[0])
        took(sq_dp.at[pl.ds(0, 7)], sq_send.at[1])
        took(r_y, r_send.at[1])
        took(r_core, r_send.at[0])
        took(r_all.at[pl.ds(0, 3 * piece)], r_send.at[2])
        took(r_all.at[pl.ds(0, half_rows)], r_send.at[3])
        for p in range(3):
            sent(p)

    return kernel


def factors(momentum, gradient, right_factor):
    hid = momentum.shape[1]
    r_rows = -(-hid // 128) * 128
    vmem = pl.BlockSpec(memory_space=pltpu.VMEM)
    hbm = pl.BlockSpec(memory_space=pl.ANY)
    return pl.pallas_call(
        make_kernel(hid, r_rows),
        out_shape=(
            pltpu.VMEM((1, hid, D), BF16),
            pltpu.VMEM((D, RANK), BF16),
            pltpu.VMEM((hid, RANK), BF16),
        ),
        in_specs=[hbm, hbm, pl.BlockSpec(memory_space=pltpu.HBM)],
        out_specs=(vmem, vmem, vmem),
        scratch_shapes=[
            pltpu.VMEM((hid, D), BF16),
            pltpu.VMEM((hid, RANK), BF16),
            pltpu.VMEM((RANK, hid), BF16),
            pltpu.VMEM((D, RANK), F32),
            pltpu.VMEM((D, RANK), F32),
            pltpu.VMEM((2 * RANK, D), BF16),
            pltpu.VMEM((RANK, D), BF16),
            pltpu.VMEM((hid, 2 * RANK), F32),
            pltpu.VMEM((2 * RANK, 2 * RANK), F32),
            pltpu.VMEM((D // 2, RANK), F32),
            pltpu.VMEM((3, D // 8, RANK), F32),
            pltpu.VMEM((3, D // 32, RANK), F32),
            pltpu.VMEM((D // 32, RANK), F32),
            pltpu.VMEM((3, D // 32, RANK), F32),
            pltpu.VMEM((r_rows, RANK), F32),
            pltpu.VMEM((r_rows // 2, RANK), F32),
            pltpu.VMEM((r_rows // 2, RANK), F32),
            pltpu.VMEM((3, r_rows // 8, RANK), F32),
            pltpu.VMEM((r_rows, RANK), BF16),
            pltpu.VMEM((RANK, RANK), F32),
            pltpu.VMEM((RANK, RANK), F32),
            pltpu.VMEM((16, 8, RANK), F32),
            pltpu.VMEM((8, 8, RANK), F32),
            pltpu.SemaphoreType.DMA((2, N_CHUNKS)),
            pltpu.SemaphoreType.DMA((1,)),
            pltpu.SemaphoreType.DMA((3, STAGES)),
            pltpu.SemaphoreType.DMA((3, STAGES)),
            pltpu.SemaphoreType.DMA((4,)),
            pltpu.SemaphoreType.DMA((4,)),
            pltpu.SemaphoreType.DMA((2,)),
            pltpu.SemaphoreType.DMA((2,)),
        ],
        compiler_params=pltpu.CompilerParams(
            collective_id=0, has_side_effects=True, vmem_limit_bytes=40 << 20
        ),
        name="factors",
    )(momentum, gradient, right_factor)


def store_kernel(momentum_ref, left_ref, next_ref, momentum_hbm, left_hbm, next_hbm, sem):
    rows = momentum_ref.shape[1] // 5
    copies = [
        pltpu.make_async_copy(
            momentum_ref.at[0, i * rows : (i + 1) * rows],
            momentum_hbm.at[0, i * rows : (i + 1) * rows],
            sem.at[i],
        )
        for i in range(5)
    ]
    copies.append(pltpu.make_async_copy(left_ref, left_hbm, sem.at[5]))
    copies.append(pltpu.make_async_copy(next_ref, next_hbm, sem.at[6]))
    for copy in copies:
        copy.start()
    for copy in copies:
        copy.wait()


def store(*outputs):
    vmem = pl.BlockSpec(memory_space=pltpu.VMEM)
    hbm = pl.BlockSpec(memory_space=pltpu.HBM)
    return pl.pallas_call(
        store_kernel,
        out_shape=tuple(jax.ShapeDtypeStruct(x.shape, x.dtype) for x in outputs),
        in_specs=[vmem] * 3,
        out_specs=(hbm,) * 3,
        scratch_shapes=[pltpu.SemaphoreType.DMA((7,))],
        compiler_params=pltpu.CompilerParams(vmem_limit_bytes=4 << 20),
        name="store",
    )(*(pltpu.with_memory_space_constraint(x, pltpu.VMEM) for x in outputs))


def shards(momentum, gradient, right_factor):
    outputs = factors(
        momentum.swapaxes(1, 2),
        gradient.swapaxes(1, 2),
        pltpu.with_memory_space_constraint(right_factor, pltpu.HBM),
    )
    momentum_next, left_factor, right_next = store(*outputs)
    return momentum_next.swapaxes(1, 2), left_factor, right_next


def solution(mesh):
    placed = (P("dp", None, "mp"), P("dp", None, "mp"), P("mp", None))
    return jax.shard_map(
        shards,
        mesh=mesh,
        in_specs=placed,
        out_specs=(P("dp", None, "mp"), P(), P("mp", None)),
        check_vma=False,
    )
```
